768 devices in a mesh: wide: 96 (over y_hi, z, core), narrow: 8 (over x, y_lo).
Axes of the slice: x: 4, y: 8 (y_hi: 4, y_lo: 2; y = y_hi * 2 + y_lo), z: 12, core: 2. Of those that a mesh axis runs over, the one named last changes fastest.
Arguments:
- embeddings: float32 [49152, 256], P(('wide', 'narrow')), may hold values from -1.5 to 1.5
- co_engagement: bfloat16 [49152, 4096], P('wide', 'narrow'), may hold values from -6 to 6
- confidence: bfloat16 [49152, 4096], P('wide', 'narrow'), may hold values from 0.099609375 to 1
- tile_offset: int32 [96, 8], P('wide', 'narrow'), may hold values from 0 to 7, each once within a row
Outputs:
- updated: float32 [49152, 256], P(('wide', 'narrow'))
The draws below stay inside these ranges and needn't reach their ends.
Inputs may be any that keep to these rules, and one draw needn't show every extreme that they name: Each row of tile_offset names each of 0 to 7 once.
All inputs are finite; a program needn't handle non-finite values.
Results may differ from the reference program's by a relative error of at most 0.0003.
Values sent between devices are 32-bit elements; how exact they have to be, the bound alone decides.
A program may use at most 32 MiB of HBM per device.

```python
import math
import jax
import jax.numpy as jnp
from jax import lax

K = 256
B = 512
ITERS = 2
DMAX = 8
BLOCKS = 96
ITEMS = 49152


def shard_levels(rng, extent, shards, low, top_value):
    level, own = 1.0, jax.random.fold_in(rng, 6)
    for dim, blocks in shards:
        heights = jnp.exp(jax.random.uniform(jax.random.fold_in(own, dim), (blocks,), jnp.float32, low / len(shards), top_value / len(shards)))
        level = level * jnp.repeat(heights, extent[dim] // blocks).reshape([-1 if axis == dim else 1 for axis in range(len(extent))])
    return level


def noise(stream_key, extent, scale, bound, shards=(), kind=jnp.bfloat16):
    array = jax.random.normal(stream_key, extent, jnp.float32) * scale
    if len(shards) > 0:
        array = shard_levels(stream_key, extent, shards, -0.22, 0.18) * array
    return jnp.clip(array, min=-bound, max=bound).astype(kind)


def setup_inputs(seed: int = 0) -> dict:
    streams_of = jax.random.split(jax.random.key(seed), 5)
    return {
        "embeddings": noise(streams_of[0], (ITEMS, K), (K ** -0.25), 1.5, ((0, 768),), jnp.float32),
        "co_engagement": noise(streams_of[1], (ITEMS, DMAX * B), 1.0, 6.0, ((0, 96), (1, 8))),
        "confidence": jnp.clip(jnp.exp(math.log(1.0) - 2.306499 * jax.random.uniform(streams_of[2], (ITEMS, DMAX * B), jnp.float32) ** shard_levels(streams_of[2], (ITEMS, DMAX * B), ((0, 96), (1, 8)), -0.2, 0.2)), 0.099609375, 1.0).astype(jnp.bfloat16),
        "tile_offset": jax.vmap(lambda own: jax.random.permutation(own, DMAX))(jax.random.split(streams_of[3], BLOCKS)).reshape((BLOCKS, DMAX)).astype(jnp.int32),
    }


def reference(embeddings, co_engagement, confidence, tile_offset):
    rate = 0.75 * math.sqrt(K) / (DMAX * B)
    x_tiles = co_engagement.reshape(BLOCKS, B, DMAX, B).transpose(0, 2, 1, 3)
    w_tiles = confidence.reshape(BLOCKS, B, DMAX, B).transpose(0, 2, 1, 3)
    partner = (jnp.arange(BLOCKS, dtype=jnp.int32)[:, None] + tile_offset + 1) % BLOCKS
    partner = partner.astype(jnp.int32)
    current = embeddings
    for step in range(ITERS):
        blocked = current.reshape(BLOCKS, B, K)

        def one_block(packed):
            own, xs, ws, parts = packed

            def one_tile(carry, tile):
                xt, wt, pidx = tile
                other = blocked[pidx]
                predicted = jnp.dot(own, other.T, precision=lax.Precision.HIGHEST, preferred_element_type=jnp.float32)
                weighted = wt.astype(jnp.float32) * (xt.astype(jnp.float32) - predicted)
                row = carry - jnp.dot(weighted, other, precision=lax.Precision.HIGHEST, preferred_element_type=jnp.float32)
                back = -jnp.dot(weighted.T, own, precision=lax.Precision.HIGHEST, preferred_element_type=jnp.float32)
                return (row, back)
            return lax.scan(one_tile, jnp.zeros((B, K), jnp.float32), (xs, ws, parts))
        rows, backs = lax.map(one_block, (blocked, x_tiles, w_tiles, partner))
        grads = rows + jax.ops.segment_sum(backs.reshape(BLOCKS * DMAX, B, K), partner.reshape(-1), num_segments=BLOCKS)
        current = current - rate * grads.reshape(ITEMS, K)
    return current
```

```python
import functools
import math

import jax
import jax.numpy as jnp
from jax import lax
from jax.experimental import pallas as pl
from jax.experimental.pallas import tpu as pltpu
from jax.sharding import PartitionSpec as P

ITERS = 2
CHUNKS = 2
MESH = pl.DeviceIdType.MESH
F32, BF16 = jnp.float32, jnp.bfloat16
NT = (((1,), (1,)), ((), ()))
TN = (((0,), (0,)), ((), ()))
NN = (((1,), (0,)), ((), ()))


def halves(a):
    hi = a.astype(BF16)
    return hi, (a - hi.astype(F32)).astype(BF16)


def dot3(a_hi, a_lo, b_hi, b_lo, dims):
    dot = functools.partial(lax.dot_general, dimension_numbers=dims, preferred_element_type=F32)
    return dot(a_hi, b_hi) + (dot(a_hi, b_lo) + dot(a_lo, b_hi))


def kernel(
    lanes, wides, rate,
    emb_ref, x_ref, c_ref, off_ref, out_ref,
    off_v, xs, cs, xr, cr, ew, near, ew_hi, ew_lo, f_hi, f_lo, w_hi, w_lo,
    back, sib_part, total, arrived, row_part, row_got,
    off_s, off_r, x_s, x_r, c_s, c_r, ag_s, ag_r, ch_s, ch_r, sb_s, sb_r,
    bs_s, bs_r, bc_s, bc_r, rs_s, rs_r,
):
    rows, width = emb_ref.shape
    block = rows * lanes
    steps = lanes // 2
    part = rows // CHUNKS
    w = lax.axis_index("wide")
    k = lax.axis_index("narrow")
    core = lax.rem(w, 2)
    below = lax.rem(w + wides - 2, wides)
    above = lax.rem(w + 2, wides)
    sibling = w + 1 - 2 * core

    def peer(r):
        return lax.rem(k + r, lanes)

    def copy(src, dst, send, recv, wide, narrow):
        return pltpu.make_async_remote_copy(
            src_ref=src, dst_ref=dst, send_sem=send, recv_sem=recv,
            device_id=(wide, narrow), device_id_type=MESH,
        )

    def over_peers(fn):
        def step(r, carry):
            fn(peer(r))
            return carry
        lax.fori_loop(1, lanes, step, 0)

    barrier = pltpu.get_barrier_semaphore()
    over_peers(lambda m: pl.semaphore_signal(barrier, inc=1, device_id=(w, m), device_id_type=MESH))
    for other in (below, above, sibling):
        pl.semaphore_signal(barrier, inc=1, device_id=(other, k), device_id_type=MESH)
    pl.semaphore_wait(barrier, lanes + 2)

    def rows_of(q):
        return pl.ds(q * part, part)

    def gather(it, m, slot):
        return copy(near.at[it, 0], ew.at[it, slot], ag_s.at[it, m], ag_r.at[it, slot], w, m)

    def chain(it, t, q):
        return copy(
            near.at[it, 2 * t, rows_of(q)], near.at[it, 2 * t + 2, rows_of(q)],
            ch_s.at[it, t, q], ch_r.at[it, t, q], below, k,
        )

    def to_sibling(it, t, q):
        return copy(
            near.at[it, 2 * t + 2 - 2 * core, rows_of(q)], near.at[it, 2 * t + 1, rows_of(q)],
            sb_s.at[it, t, q], sb_r.at[it, t, q], sibling, k,
        )

    def offsets(m, slot):
        return copy(off_v.at[k], off_v.at[slot], off_s.at[m], off_r.at[slot], w, m)

    def x_copy(m, slot):
        return copy(xs.at[m], xr.at[slot], x_s.at[m], x_r.at[slot], w, m)

    def c_copy(m, slot):
        return copy(cs.at[m], cr.at[slot], c_s.at[m], c_r.at[slot], w, m)

    def back_sibling(it, t):
        return copy(
            back.at[it, 2 * t], sib_part.at[it, t + core], bs_s.at[it, t], bs_r.at[it, t], sibling, k
        )

    def back_chain(it, v, q):
        return copy(
            total.at[it, v, rows_of(q)], arrived.at[it, v, rows_of(q)],
            bc_s.at[it, v, q], bc_r.at[it, v, q], above, k,
        )

    def scatter(it, m, slot):
        return copy(row_part.at[it, m], row_got.at[it, slot], rs_s.at[it, m], rs_r.at[it, slot], w, m)

    def start_forward(it, value):
        near[it, 0] = value
        ew[it, k] = value
        for q in range(CHUNKS):
            chain(it, 0, q).start()

        @pl.when(core == 1)
        def _():
            for q in range(CHUNKS):
                to_sibling(it, 0, q).start()

        over_peers(lambda m: gather(it, m, k).start())

    def forward(it, u):
        for q in range(CHUNKS):
            chain(it, u - 1, q).wait_recv()
            if u < steps:
                chain(it, u, q).start()
                to_sibling(it, u - 1 + core, q).start()
            else:
                @pl.when(core == 0)
                def _():
                    to_sibling(it, steps - 1, q).start()

    def wait_gather(it):
        over_peers(lambda m: gather(it, m, m).wait_recv())
        hi, lo = halves(ew[it].reshape(block, width))
        ew_hi[...] = hi
        ew_lo[...] = lo

    def tile(it, u, slot_of):
        for q in range(CHUNKS):
            to_sibling(it, u - 1, q).wait_recv()
        lo_row = (2 * u - 2) * rows
        both = pl.ds(lo_row, 2 * rows)
        f = near[it, 2 * u - 1:2 * u + 1].reshape(2 * rows, width)
        fh, fl = halves(f)
        f_hi[both] = fh
        f_lo[both] = fl
        predicted = dot3(fh, fl, ew_hi[...], ew_lo[...], NT)
        for i in range(2):
            slot = slot_of[2 * u - 2 + i]
            weighted = cr[slot] * (xr[slot] - predicted[i * rows:(i + 1) * rows])
            wh, wl = halves(weighted)
            w_hi[pl.ds(lo_row + i * rows, rows)] = wh
            w_lo[pl.ds(lo_row + i * rows, rows)] = wl
        out = dot3(w_hi[both], w_lo[both], ew_hi[...], ew_lo[...], NN)
        back[it, 2 * u - 2] = out[:rows]
        back[it, 2 * u - 1] = out[rows:]
        back_sibling(it, u - 1).start()

    def wait_sibling_part(it, u):
        if u == steps:
            @pl.when(core == 0)
            def _():
                back_sibling(it, steps - 1).wait_recv()
        elif u == 0:
            @pl.when(core == 1)
            def _():
                back_sibling(it, 0).wait_recv()
        else:
            back_sibling(it, u - 1 + core).wait_recv()

    def backward(it, v):
        u = steps - v
        wait_sibling_part(it, u)
        for q in range(CHUNKS):
            here = rows_of(q)
            if v > 0:
                back_chain(it, v - 1, q).wait_recv()
            value = back[it, 2 * u - 1, here] + sib_part[it, u, here]
            if v > 0:
                value = value + arrived[it, v - 1, here]
            total[it, v, here] = value
            back_chain(it, v, q).start()

    def row_terms(it):
        terms = dot3(w_hi[...], w_lo[...], f_hi[...], f_lo[...], TN)
        row_part[it] = terms.reshape(lanes, rows, width)
        row_got[it, k] = row_part[it, k]
        over_peers(lambda m: scatter(it, m, k).start())

    def finish(it):
        over_peers(lambda m: scatter(it, m, m).wait_recv())
        grad = row_got[it, 0]
        for m in range(1, lanes):
            grad = grad + row_got[it, m]
        wait_sibling_part(it, 0)
        grad = grad + sib_part[it, 0]
        for q in range(CHUNKS):
            back_chain(it, steps - 1, q).wait_recv()
        grad = grad + arrived[it, steps - 1]
        return near[it, 0] + rate * grad

    off_v[k] = jnp.full(off_v.shape[1:], off_ref[0, 0], jnp.int32)
    start_forward(0, emb_ref[...])
    over_peers(lambda m: offsets(m, k).start())

    def transposed(m, ref):
        pick = (
            lax.broadcasted_iota(jnp.int32, (rows, block), 1)
            == lax.broadcasted_iota(jnp.int32, (rows, block), 0) + m * rows
        )
        pick = jnp.where(pick, 1.0, 0.0).astype(BF16)
        return lax.dot_general(pick, ref[...], NT, preferred_element_type=F32)

    def send_tiles(m):
        xs[m] = transposed(m, x_ref)
        x_copy(m, k).start()
        cs[m] = transposed(m, c_ref)
        c_copy(m, k).start()

    over_peers(send_tiles)
    xr[k] = transposed(k, x_ref)
    cr[k] = transposed(k, c_ref)
    for it in range(ITERS):
        sib_part[it, steps * core] = jnp.zeros((rows, width), F32)

    for it in range(ITERS):
        if it == 0:
            for u in range(1, steps + 1):
                forward(it, u)
            wait_gather(it)
            over_peers(lambda m: offsets(m, m).wait_recv())
            offs = [jnp.max(off_v[s]) for s in range(lanes)]
            slot_of = []
            for d in range(lanes):
                found = jnp.int32(0)
                for s in range(1, lanes):
                    found = jnp.where(offs[s] == d, s, found)
                slot_of.append(found)
            over_peers(lambda m: x_copy(m, m).wait_recv())
            over_peers(lambda m: c_copy(m, m).wait_recv())
            tile(it, steps, slot_of)
            backward(it, 0)
            for u in range(steps - 1, 0, -1):
                tile(it, u, slot_of)
        else:
            for u in range(1, steps // 2 + 1):
                forward(it, u)
            wait_gather(it)
            for u in range(1, steps // 2 + 1):
                tile(it, u, slot_of)
            for u in range(steps // 2 + 1, steps + 1):
                forward(it, u)
                tile(it, u, slot_of)
            backward(it, 0)
        row_terms(it)
        for v in range(1, steps):
            backward(it, v)
        value = finish(it)
        if it < ITERS - 1:
            start_forward(it + 1, value)
        else:
            out_ref[...] = value

    def drain(m):
        offsets(m, k).wait_send()
        x_copy(m, k).wait_send()
        c_copy(m, k).wait_send()
        for it in range(ITERS):
            gather(it, m, k).wait_send()
            scatter(it, m, k).wait_send()

    over_peers(drain)
    for it in range(ITERS):
        for t in range(steps):
            back_sibling(it, t).wait_send()
            for q in range(CHUNKS):
                chain(it, t, q).wait_send()
                to_sibling(it, t, q).wait_send()
                back_chain(it, t, q).wait_send()


def body(embeddings, co_engagement, confidence, tile_offset):
    rows, width = embeddings.shape
    lanes = lax.axis_size("narrow")
    wides = lax.axis_size("wide")
    block = rows * lanes
    steps = lanes // 2
    rate = 0.75 * math.sqrt(width) / (lanes * block)
    vmem = pl.BlockSpec(memory_space=pltpu.VMEM)
    dma = pltpu.SemaphoreType.DMA
    return pl.pallas_call(
        functools.partial(kernel, lanes, wides, rate),
        out_shape=jax.ShapeDtypeStruct((rows, width), F32),
        in_specs=[vmem, vmem, vmem, pl.BlockSpec(memory_space=pltpu.SMEM)],
        out_specs=vmem,
        scratch_shapes=[
            pltpu.VMEM((lanes, 8, 128), jnp.int32),
            *[pltpu.VMEM((lanes, rows, block), F32)] * 4,
            pltpu.VMEM((ITERS, lanes, rows, width), F32),
            pltpu.VMEM((ITERS, lanes + 1, rows, width), F32),
            *[pltpu.VMEM((block, width), BF16)] * 4,
            *[pltpu.VMEM((block, block), BF16)] * 2,
            pltpu.VMEM((ITERS, lanes, rows, width), F32),
            pltpu.VMEM((ITERS, steps + 1, rows, width), F32),
            pltpu.VMEM((ITERS, steps, rows, width), F32),
            pltpu.VMEM((ITERS, steps, rows, width), F32),
            pltpu.VMEM((ITERS, lanes, rows, width), F32),
            pltpu.VMEM((ITERS, lanes, rows, width), F32),
            *[dma((lanes,))] * 6,
            *[dma((ITERS, lanes))] * 2,
            *[dma((ITERS, steps, CHUNKS))] * 4,
            *[dma((ITERS, steps))] * 2,
            *[dma((ITERS, steps, CHUNKS))] * 2,
            *[dma((ITERS, lanes))] * 2,
        ],
        compiler_params=pltpu.CompilerParams(
            collective_id=0, has_side_effects=True, vmem_limit_bytes=40 * 1024 * 1024
        ),
        cost_estimate=pl.CostEstimate(
            flops=ITERS * 18 * block * block * width, bytes_accessed=4 * block * block, transcendentals=0
        ),
    )(embeddings, co_engagement, confidence, tile_offset)


def solution(mesh):
    in_specs = (
        P(("wide", "narrow"), None),
        P("wide", "narrow"),
        P("wide", "narrow"),
        P("wide", "narrow"),
    )
    out_specs = P(("wide", "narrow"), None)
    return jax.shard_map(body, mesh=mesh, in_specs=in_specs, out_specs=out_specs, check_vma=False)
```

```python
import functools
import math

import jax
import jax.numpy as jnp
from jax import lax
from jax.experimental import pallas as pl
from jax.experimental.pallas import tpu as pltpu
from jax.sharding import PartitionSpec as P

ITERS = 2
CHUNKS = 2
MESH = pl.DeviceIdType.MESH
F32, BF16 = jnp.float32, jnp.bfloat16
NT = (((1,), (1,)), ((), ()))
TN = (((0,), (0,)), ((), ()))
NN = (((1,), (0,)), ((), ()))


def halves(a):
    hi = a.astype(BF16)
    return hi, (a - hi.astype(F32)).astype(BF16)


def dot3(a_hi, a_lo, b_hi, b_lo, dims):
    dot = functools.partial(lax.dot_general, dimension_numbers=dims, preferred_element_type=F32)
    return dot(a_hi, b_hi) + (dot(a_hi, b_lo) + dot(a_lo, b_hi))


def kernel(
    lanes, wides, rate,
    emb_ref, x_ref, c_ref, off_ref, out_ref,
    off_v, xs, cs, xr, cr, ew, near, ew_hi, ew_lo, f_hi, f_lo, w_hi, w_lo,
    back, sib_part, total, arrived, row_part, row_got, x_in, c_in, pred,
    in_s, off_s, off_r, x_s, x_r, c_s, c_r, ag_s, ag_r, ch_s, ch_r, sb_s, sb_r,
    bs_s, bs_r, bc_s, bc_r, rs_s, rs_r,
):
    rows, width = emb_ref.shape
    block = rows * lanes
    steps = lanes // 2
    part = rows // CHUNKS
    w = lax.axis_index("wide")
    k = lax.axis_index("narrow")
    core = lax.rem(w, 2)
    below = lax.rem(w + wides - 2, wides)
    above = lax.rem(w + 2, wides)
    sibling = w + 1 - 2 * core

    def peer(r):
        return lax.rem(k + r, lanes)

    def copy(src, dst, send, recv, wide, narrow):
        return pltpu.make_async_remote_copy(
            src_ref=src, dst_ref=dst, send_sem=send, recv_sem=recv,
            device_id=(wide, narrow), device_id_type=MESH,
        )

    def over_peers(fn):
        def step(r, carry):
            fn(peer(r))
            return carry
        lax.fori_loop(1, lanes, step, 0)

    e_load = pltpu.make_async_copy(emb_ref, near.at[0, 0], in_s.at[0])
    x_load = pltpu.make_async_copy(x_ref, x_in, in_s.at[1])
    c_load = pltpu.make_async_copy(c_ref, c_in, in_s.at[2])
    barrier = pltpu.get_barrier_semaphore()
    over_peers(lambda m: pl.semaphore_signal(barrier, inc=1, device_id=(w, m), device_id_type=MESH))
    for other in (below, above, sibling):
        pl.semaphore_signal(barrier, inc=1, device_id=(other, k), device_id_type=MESH)
    e_load.start()
    x_load.start()
    c_load.start()
    off_v[k] = jnp.full(off_v.shape[1:], off_ref[0, 0], jnp.int32)
    for it in range(ITERS):
        sib_part[it, steps * core] = jnp.zeros((rows, width), F32)
    e_load.wait()
    pl.semaphore_wait(barrier, lanes + 2)

    def rows_of(q):
        return pl.ds(q * part, part)

    def gather(it, i, m, piece):
        src = near.at[it, 0] if i < lanes // 2 else ew.at[it, piece]
        return copy(src, ew.at[it, piece], ag_s.at[it, i], ag_r.at[it, piece], w, m)

    neighbour = k + 1 - 2 * lax.rem(k, 2)

    def pass_on(it):
        gather(it, 0, neighbour, neighbour).wait_recv()
        for i in range(1, lanes // 2):
            gather(it, lanes // 2 - 1 + i, peer(2 * i), neighbour).start()

    def chain(it, t, q):
        return copy(
            near.at[it, 2 * t, rows_of(q)], near.at[it, 2 * t + 2, rows_of(q)],
            ch_s.at[it, t, q], ch_r.at[it, t, q], below, k,
        )

    def to_sibling(it, t, q):
        return copy(
            near.at[it, 2 * t + 2 - 2 * core, rows_of(q)], near.at[it, 2 * t + 1, rows_of(q)],
            sb_s.at[it, t, q], sb_r.at[it, t, q], sibling, k,
        )

    def offsets(m, slot):
        return copy(off_v.at[k], off_v.at[slot], off_s.at[m], off_r.at[slot], w, m)

    def x_copy(m, slot):
        return copy(xs.at[m], xr.at[slot], x_s.at[m], x_r.at[slot], w, m)

    def c_copy(m, slot):
        return copy(cs.at[m], cr.at[slot], c_s.at[m], c_r.at[slot], w, m)

    def back_sibling(it, t):
        return copy(
            back.at[it, 2 * t], sib_part.at[it, t + core], bs_s.at[it, t], bs_r.at[it, t], sibling, k
        )

    def back_chain(it, v, q):
        return copy(
            total.at[it, v, rows_of(q)], arrived.at[it, v, rows_of(q)],
            bc_s.at[it, v, q], bc_r.at[it, v, q], above, k,
        )

    def scatter(it, m, slot):
        return copy(row_part.at[it, m], row_got.at[it, slot], rs_s.at[it, m], rs_r.at[it, slot], w, m)

    def start_forward(it):
        for q in range(CHUNKS):
            chain(it, 0, q).start()

        @pl.when(core == 1)
        def _():
            for q in range(CHUNKS):
                to_sibling(it, 0, q).start()

        for i in range(lanes // 2):
            gather(it, i, peer(2 * i) if i else neighbour, k).start()
        ew[it, k] = near[it, 0]

    def forward(it, u):
        for q in range(CHUNKS):
            chain(it, u - 1, q).wait_recv()
            if u < steps:
                chain(it, u, q).start()
                to_sibling(it, u - 1 + core, q).start()
            else:
                @pl.when(core == 0)
                def _():
                    to_sibling(it, steps - 1, q).start()

    def wait_gather(it):
        over_peers(
            lambda m: pl.when(m != neighbour)(lambda: gather(it, 1, m, m).wait_recv())
        )
        hi, lo = halves(ew[it].reshape(block, width))
        ew_hi[...] = hi
        ew_lo[...] = lo

    def predict(it, first, last):
        for t in range(first - 1, last):
            for q in range(CHUNKS):
                to_sibling(it, t, q).wait_recv()
        some = pl.ds((2 * first - 2) * rows, 2 * (last - first + 1) * rows)
        fh, fl = halves(near[it, 2 * first - 1:2 * last + 1].reshape(some.size, width))
        f_hi[some] = fh
        f_lo[some] = fl
        pred[some] = dot3(fh, fl, ew_hi[...], ew_lo[...], NT)

    def tile(it, first, last, slot_of):
        some = pl.ds((2 * first - 2) * rows, 2 * (last - first + 1) * rows)
        for d in range(2 * first - 2, 2 * last):
            here = pl.ds(d * rows, rows)
            wh, wl = halves(cr[slot_of[d]] * (xr[slot_of[d]] - pred[here]))
            w_hi[here] = wh
            w_lo[here] = wl
        out = dot3(w_hi[some], w_lo[some], ew_hi[...], ew_lo[...], NN)
        back[it, 2 * first - 2:2 * last] = out.reshape(2 * (last - first + 1), rows, width)
        for u in range(first, last + 1):
            back_sibling(it, u - 1).start()

    def wait_sibling_part(it, u):
        if u == steps:
            @pl.when(core == 0)
            def _():
                back_sibling(it, steps - 1).wait_recv()
        elif u == 0:
            @pl.when(core == 1)
            def _():
                back_sibling(it, 0).wait_recv()
        else:
            back_sibling(it, u - 1 + core).wait_recv()

    def backward(it, v):
        u = steps - v
        wait_sibling_part(it, u)
        for q in range(CHUNKS):
            here = rows_of(q)
            if v > 0:
                back_chain(it, v - 1, q).wait_recv()
            value = back[it, 2 * u - 1, here] + sib_part[it, u, here]
            if v > 0:
                value = value + arrived[it, v - 1, here]
            total[it, v, here] = value
            back_chain(it, v, q).start()

    def row_terms(it):
        terms = dot3(w_hi[...], w_lo[...], f_hi[...], f_lo[...], TN)
        row_part[it] = terms.reshape(lanes, rows, width)
        row_got[it, k] = row_part[it, k]
        over_peers(lambda m: scatter(it, m, k).start())

    def finish(it, store):
        over_peers(lambda m: scatter(it, m, m).wait_recv())
        wait_sibling_part(it, 0)
        grad = row_got[it, 0] + sib_part[it, 0]
        for m in range(1, lanes):
            grad = grad + row_got[it, m]
        for q in range(CHUNKS):
            here = rows_of(q)
            back_chain(it, steps - 1, q).wait_recv()
            store(here, near[it, 0, here] + rate * (grad[q * part:(q + 1) * part] + arrived[it, steps - 1, here]))

    def keep(here, value):
        near[1, 0, here] = value

    def result(here, value):
        out_ref[here] = value

    start_forward(0)
    over_peers(lambda m: offsets(m, k).start())

    def transpose(ref, out):
        eye = (
            lax.broadcasted_iota(jnp.int32, (block, block), 0)
            == lax.broadcasted_iota(jnp.int32, (block, block), 1)
        )
        eye = jnp.where(eye, 1.0, 0.0).astype(BF16)
        out[...] = lax.dot_general(eye, ref[...], NT, preferred_element_type=F32).reshape(out.shape)

    x_load.wait()
    transpose(x_in, xs)
    over_peers(lambda m: x_copy(m, k).start())
    c_load.wait()
    transpose(c_in, cs)
    pass_on(0)
    over_peers(lambda m: c_copy(m, k).start())
    xr[k] = xs[k]
    cr[k] = cs[k]

    for it in range(ITERS):
        if it == 0:
            for u in range(1, steps + 1):
                forward(it, u)
            wait_gather(it)
            predict(it, 1, steps)
            over_peers(lambda m: offsets(m, m).wait_recv())
            offs = [jnp.max(off_v[s]) for s in range(lanes)]
            slot_of = []
            for d in range(lanes):
                found = jnp.int32(0)
                for s in range(1, lanes):
                    found = jnp.where(offs[s] == d, s, found)
                slot_of.append(found)
            over_peers(lambda m: x_copy(m, m).wait_recv())
            over_peers(lambda m: c_copy(m, m).wait_recv())
            tile(it, steps, steps, slot_of)
            tile(it, 1, steps - 1, slot_of)
        else:
            pass_on(it)
            for u in range(1, steps + 1):
                forward(it, u)
                if u == 2:
                    wait_gather(it)
                    predict(it, 1, 1)
                    tile(it, 1, 1, slot_of)
                if u >= 2:
                    predict(it, u, u)
                    tile(it, u, u, slot_of)
        backward(it, 0)
        row_terms(it)
        for v in range(1, steps):
            backward(it, v)
        finish(it, keep if it < ITERS - 1 else result)
        if it < ITERS - 1:
            start_forward(it + 1)

    def drain(m):
        offsets(m, k).wait_send()
        x_copy(m, k).wait_send()
        c_copy(m, k).wait_send()
        for it in range(ITERS):
            scatter(it, m, k).wait_send()

    over_peers(drain)
    for it in range(ITERS):
        for i in range(lanes - 1):
            gather(it, i, neighbour, k if i < lanes // 2 else neighbour).wait_send()
        for t in range(steps):
            back_sibling(it, t).wait_send()
            for q in range(CHUNKS):
                chain(it, t, q).wait_send()
                to_sibling(it, t, q).wait_send()
                back_chain(it, t, q).wait_send()


def body(embeddings, co_engagement, confidence, tile_offset):
    rows, width = embeddings.shape
    lanes = lax.axis_size("narrow")
    wides = lax.axis_size("wide")
    block = rows * lanes
    steps = lanes // 2
    rate = 0.75 * math.sqrt(width) / (lanes * block)
    vmem = pl.BlockSpec(memory_space=pltpu.VMEM)
    hbm = pl.BlockSpec(memory_space=pltpu.HBM)
    dma = pltpu.SemaphoreType.DMA
    return pl.pallas_call(
        functools.partial(kernel, lanes, wides, rate),
        out_shape=jax.ShapeDtypeStruct((rows, width), F32),
        in_specs=[hbm, hbm, hbm, pl.BlockSpec(memory_space=pltpu.SMEM)],
        out_specs=vmem,
        scratch_shapes=[
            pltpu.VMEM((lanes, 8, 128), jnp.int32),
            *[pltpu.VMEM((lanes, rows, block), F32)] * 4,
            pltpu.VMEM((ITERS, lanes, rows, width), F32),
            pltpu.VMEM((ITERS, lanes + 1, rows, width), F32),
            *[pltpu.VMEM((block, width), BF16)] * 4,
            *[pltpu.VMEM((block, block), BF16)] * 2,
            pltpu.VMEM((ITERS, lanes, rows, width), F32),
            pltpu.VMEM((ITERS, steps + 1, rows, width), F32),
            pltpu.VMEM((ITERS, steps, rows, width), F32),
            pltpu.VMEM((ITERS, steps, rows, width), F32),
            pltpu.VMEM((ITERS, lanes, rows, width), F32),
            pltpu.VMEM((ITERS, lanes, rows, width), F32),
            *[pltpu.VMEM((block, block), BF16)] * 2,
            pltpu.VMEM((block, block), F32),
            dma((3,)),
            *[dma((lanes,))] * 6,
            *[dma((ITERS, lanes))] * 2,
            *[dma((ITERS, steps, CHUNKS))] * 4,
            *[dma((ITERS, steps))] * 2,
            *[dma((ITERS, steps, CHUNKS))] * 2,
            *[dma((ITERS, lanes))] * 2,
        ],
        compiler_params=pltpu.CompilerParams(
            collective_id=0, has_side_effects=True, vmem_limit_bytes=63 * 1024 * 1024
        ),
        cost_estimate=pl.CostEstimate(
            flops=ITERS * 18 * block * block * width, bytes_accessed=4 * block * block, transcendentals=0
        ),
    )(embeddings, co_engagement, confidence, tile_offset)


def solution(mesh):
    in_specs = (
        P(("wide", "narrow"), None),
        P("wide", "narrow"),
        P("wide", "narrow"),
        P("wide", "narrow"),
    )
    out_specs = P(("wide", "narrow"), None)
    return jax.shard_map(body, mesh=mesh, in_specs=in_specs, out_specs=out_specs, check_vma=False)
```

```python
import functools
import math

import jax
import jax.numpy as jnp
from jax import lax
from jax.experimental import pallas as pl
from jax.experimental.pallas import tpu as pltpu
from jax.sharding import PartitionSpec as P

ITERS = 2
CHUNKS = 1
HOP = {1: 1, 2: 2, 3: 1, 4: 2}
MESH = pl.DeviceIdType.MESH
F32, BF16 = jnp.float32, jnp.bfloat16
NT = (((1,), (1,)), ((), ()))
TN = (((0,), (0,)), ((), ()))
NN = (((1,), (0,)), ((), ()))


def halves(a):
    hi = a.astype(BF16)
    return hi, (a - hi.astype(F32)).astype(BF16)


def dot3(a_hi, a_lo, b_hi, b_lo, dims):
    dot = functools.partial(lax.dot_general, dimension_numbers=dims, preferred_element_type=F32)
    return dot(a_hi, b_hi) + (dot(a_hi, b_lo) + dot(a_lo, b_hi))


def kernel(
    lanes, wides, rate,
    emb_ref, x_ref, c_ref, off_ref, out_ref,
    off_v, xs, cs, xr, cr, ew, near, ew_hi, ew_lo, f_hi, f_lo, w_hi, w_lo,
    back, sib_part, total, arrived, row_part, row_got, x_in, c_in, pred,
    in_s, off_s, off_r, x_s, x_r, c_s, c_r, ag_s, ag_r, ch_s, ch_r, sb_s, sb_r,
    bs_s, bs_r, bc_s, bc_r, rs_s, rs_r,
):
    rows, width = emb_ref.shape
    block = rows * lanes
    steps = lanes // 2
    part = rows // CHUNKS
    w = lax.axis_index("wide")
    k = lax.axis_index("narrow")
    core = lax.rem(w, 2)
    below = {g: lax.rem(w + wides - 2 * g, wides) for g in (1, 2)}
    above = {g: lax.rem(w + 2 * g, wides) for g in (1, 2)}
    sibling = w + 1 - 2 * core

    def peer(r):
        return lax.rem(k + r, lanes)

    def copy(src, dst, send, recv, wide, narrow):
        return pltpu.make_async_remote_copy(
            src_ref=src, dst_ref=dst, send_sem=send, recv_sem=recv,
            device_id=(wide, narrow), device_id_type=MESH,
        )

    def over_peers(fn):
        def step(r, carry):
            fn(peer(r))
            return carry
        lax.fori_loop(1, lanes, step, 0)

    e_load = pltpu.make_async_copy(emb_ref, near.at[0, 0], in_s.at[0])
    x_load = pltpu.make_async_copy(x_ref, x_in, in_s.at[1])
    c_load = pltpu.make_async_copy(c_ref, c_in, in_s.at[2])
    barrier = pltpu.get_barrier_semaphore()
    over_peers(lambda m: pl.semaphore_signal(barrier, inc=1, device_id=(w, m), device_id_type=MESH))
    for other in (*below.values(), *above.values(), sibling):
        pl.semaphore_signal(barrier, inc=1, device_id=(other, k), device_id_type=MESH)
    e_load.start()
    x_load.start()
    c_load.start()
    off_v[k] = jnp.full(off_v.shape[1:], off_ref[0, 0], jnp.int32)
    for it in range(ITERS):
        sib_part[it, steps * core] = jnp.zeros((rows, width), F32)
    e_load.wait()
    pl.semaphore_wait(barrier, lanes + 4)

    def rows_of(q):
        return pl.ds(q * part, part)

    def gather(it, i, m, piece):
        src = near.at[it, 0] if i < lanes // 2 else ew.at[it, piece]
        return copy(src, ew.at[it, piece], ag_s.at[it, i], ag_r.at[it, piece], w, m)

    neighbour = k + 1 - 2 * lax.rem(k, 2)

    def pass_on(it):
        gather(it, 0, neighbour, neighbour).wait_recv()
        for i in range(1, lanes // 2):
            gather(it, lanes // 2 - 1 + i, peer(2 * i), neighbour).start()

    def down(it, h, q):
        return copy(
            near.at[it, 2 * (h - HOP[h]), rows_of(q)], near.at[it, 2 * h, rows_of(q)],
            ch_s.at[it, h - 1, q], ch_r.at[it, h - 1, q], below[HOP[h]], k,
        )

    def to_sibling(it, t, q):
        return copy(
            near.at[it, 2 * t + 2 - 2 * core, rows_of(q)], near.at[it, 2 * t + 1, rows_of(q)],
            sb_s.at[it, t, q], sb_r.at[it, t, q], sibling, k,
        )

    def offsets(m, slot):
        return copy(off_v.at[k], off_v.at[slot], off_s.at[m], off_r.at[slot], w, m)

    def x_copy(m, slot):
        return copy(xs.at[m], xr.at[slot], x_s.at[m], x_r.at[slot], w, m)

    def c_copy(m, slot):
        return copy(cs.at[m], cr.at[slot], c_s.at[m], c_r.at[slot], w, m)

    def back_sibling(it, t):
        return copy(
            back.at[it, 2 * t], sib_part.at[it, t + core], bs_s.at[it, t], bs_r.at[it, t], sibling, k
        )

    def up(it, h, q):
        return copy(
            total.at[it, h - 1, rows_of(q)], arrived.at[it, h - 1, rows_of(q)],
            bc_s.at[it, h - 1, q], bc_r.at[it, h - 1, q], above[HOP[h]], k,
        )

    def scatter(it, m, slot):
        return copy(row_part.at[it, m], row_got.at[it, slot], rs_s.at[it, m], rs_r.at[it, slot], w, m)

    def start_forward(it):
        for h in (2, 1):
            for q in range(CHUNKS):
                down(it, h, q).start()

        @pl.when(core == 1)
        def _():
            for q in range(CHUNKS):
                to_sibling(it, 0, q).start()

        for i in range(lanes // 2):
            gather(it, i, peer(2 * i) if i else neighbour, k).start()
        ew[it, k] = near[it, 0]

    def forward(it, u):
        for q in range(CHUNKS):
            down(it, u, q).wait_recv()
            if u == 2:
                down(it, 4, q).start()
                down(it, 3, q).start()
            if u < steps:
                to_sibling(it, u - 1 + core, q).start()
            else:
                @pl.when(core == 0)
                def _():
                    to_sibling(it, steps - 1, q).start()

    def wait_gather(it):
        over_peers(
            lambda m: pl.when(m != neighbour)(lambda: gather(it, 1, m, m).wait_recv())
        )
        hi, lo = halves(ew[it].reshape(block, width))
        ew_hi[...] = hi
        ew_lo[...] = lo

    def predict(it, first, last):
        for t in range(first - 1, last):
            for q in range(CHUNKS):
                to_sibling(it, t, q).wait_recv()
        some = pl.ds((2 * first - 2) * rows, 2 * (last - first + 1) * rows)
        fh, fl = halves(near[it, 2 * first - 1:2 * last + 1].reshape(some.size, width))
        f_hi[some] = fh
        f_lo[some] = fl
        pred[some] = dot3(fh, fl, ew_hi[...], ew_lo[...], NT)

    def tile(it, first, last, slot_of):
        some = pl.ds((2 * first - 2) * rows, 2 * (last - first + 1) * rows)
        for d in range(2 * first - 2, 2 * last):
            here = pl.ds(d * rows, rows)
            wh, wl = halves(cr[slot_of[d]] * (xr[slot_of[d]] - pred[here]))
            w_hi[here] = wh
            w_lo[here] = wl
        out = dot3(w_hi[some], w_lo[some], ew_hi[...], ew_lo[...], NN)
        back[it, 2 * first - 2:2 * last] = out.reshape(2 * (last - first + 1), rows, width)
        for u in range(first, last + 1):
            back_sibling(it, u - 1).start()

    def wait_sibling_part(it, u):
        if u == steps:
            @pl.when(core == 0)
            def _():
                back_sibling(it, steps - 1).wait_recv()
        elif u == 0:
            @pl.when(core == 1)
            def _():
                back_sibling(it, 0).wait_recv()
        else:
            back_sibling(it, u - 1 + core).wait_recv()

    def backward(it, h):
        wait_sibling_part(it, h)
        for q in range(CHUNKS):
            here = rows_of(q)
            value = back[it, 2 * h - 1, here] + sib_part[it, h, here]
            if h == 2:
                for far in (3, 4):
                    up(it, far, q).wait_recv()
                    value = value + arrived[it, far - 1, here]
            total[it, h - 1, here] = value
            up(it, h, q).start()

    def row_terms(it):
        terms = dot3(w_hi[...], w_lo[...], f_hi[...], f_lo[...], TN)
        row_part[it] = terms.reshape(lanes, rows, width)
        row_got[it, k] = row_part[it, k]
        over_peers(lambda m: scatter(it, m, k).start())

    def finish(it, store):
        over_peers(lambda m: scatter(it, m, m).wait_recv())
        wait_sibling_part(it, 0)
        grad = row_got[it, 0] + sib_part[it, 0]
        for m in range(1, lanes):
            grad = grad + row_got[it, m]
        for q in range(CHUNKS):
            here = rows_of(q)
            terms = grad[q * part:(q + 1) * part]
            for h in (1, 2):
                up(it, h, q).wait_recv()
                terms = terms + arrived[it, h - 1, here]
            store(here, near[it, 0, here] + rate * terms)

    def keep(here, value):
        near[1, 0, here] = value

    def result(here, value):
        out_ref[here] = value

    start_forward(0)
    over_peers(lambda m: offsets(m, k).start())

    def transpose(ref, out):
        eye = (
            lax.broadcasted_iota(jnp.int32, (block, block), 0)
            == lax.broadcasted_iota(jnp.int32, (block, block), 1)
        )
        eye = jnp.where(eye, 1.0, 0.0).astype(BF16)
        out[...] = lax.dot_general(eye, ref[...], NT, preferred_element_type=F32).reshape(out.shape)

    x_load.wait()
    transpose(x_in, xs)
    over_peers(lambda m: x_copy(m, k).start())
    c_load.wait()
    transpose(c_in, cs)
    pass_on(0)
    over_peers(lambda m: c_copy(m, k).start())
    xr[k] = xs[k]
    cr[k] = cs[k]

    for it in range(ITERS):
        if it == 0:
            for u in (2, 1, 3, 4):
                forward(it, u)
            wait_gather(it)
            predict(it, 1, steps)
            over_peers(lambda m: offsets(m, m).wait_recv())
            offs = [jnp.max(off_v[s]) for s in range(lanes)]
            slot_of = []
            for d in range(lanes):
                found = jnp.int32(0)
                for s in range(1, lanes):
                    found = jnp.where(offs[s] == d, s, found)
                slot_of.append(found)
            over_peers(lambda m: x_copy(m, m).wait_recv())
            over_peers(lambda m: c_copy(m, m).wait_recv())
            tile(it, steps, steps, slot_of)
            tile(it, 1, steps - 1, slot_of)
        else:
            pass_on(it)
            forward(it, 2)
            forward(it, 1)
            wait_gather(it)
            predict(it, 1, 2)
            tile(it, 1, 2, slot_of)
            forward(it, 3)
            forward(it, 4)
            predict(it, 3, 4)
            tile(it, 3, 4, slot_of)
        backward(it, 4)
        backward(it, 3)
        backward(it, 1)
        row_terms(it)
        backward(it, 2)
        finish(it, keep if it < ITERS - 1 else result)
        if it < ITERS - 1:
            start_forward(it + 1)

    def drain(m):
        offsets(m, k).wait_send()
        x_copy(m, k).wait_send()
        c_copy(m, k).wait_send()
        for it in range(ITERS):
            scatter(it, m, k).wait_send()

    over_peers(drain)
    for it in range(ITERS):
        for i in range(lanes - 1):
            gather(it, i, neighbour, k if i < lanes // 2 else neighbour).wait_send()
        for t in range(steps):
            back_sibling(it, t).wait_send()
            for q in range(CHUNKS):
                down(it, t + 1, q).wait_send()
                to_sibling(it, t, q).wait_send()
                up(it, t + 1, q).wait_send()


def body(embeddings, co_engagement, confidence, tile_offset):
    rows, width = embeddings.shape
    lanes = lax.axis_size("narrow")
    wides = lax.axis_size("wide")
    block = rows * lanes
    steps = lanes // 2
    rate = 0.75 * math.sqrt(width) / (lanes * block)
    vmem = pl.BlockSpec(memory_space=pltpu.VMEM)
    hbm = pl.BlockSpec(memory_space=pltpu.HBM)
    dma = pltpu.SemaphoreType.DMA
    return pl.pallas_call(
        functools.partial(kernel, lanes, wides, rate),
        out_shape=jax.ShapeDtypeStruct((rows, width), F32),
        in_specs=[hbm, hbm, hbm, pl.BlockSpec(memory_space=pltpu.SMEM)],
        out_specs=vmem,
        scratch_shapes=[
            pltpu.VMEM((lanes, 8, 128), jnp.int32),
            *[pltpu.VMEM((lanes, rows, block), F32)] * 4,
            pltpu.VMEM((ITERS, lanes, rows, width), F32),
            pltpu.VMEM((ITERS, lanes + 1, rows, width), F32),
            *[pltpu.VMEM((block, width), BF16)] * 4,
            *[pltpu.VMEM((block, block), BF16)] * 2,
            pltpu.VMEM((ITERS, lanes, rows, width), F32),
            pltpu.VMEM((ITERS, steps + 1, rows, width), F32),
            pltpu.VMEM((ITERS, steps, rows, width), F32),
            pltpu.VMEM((ITERS, steps, rows, width), F32),
            pltpu.VMEM((ITERS, lanes, rows, width), F32),
            pltpu.VMEM((ITERS, lanes, rows, width), F32),
            *[pltpu.VMEM((block, block), BF16)] * 2,
            pltpu.VMEM((block, block), F32),
            dma((3,)),
            *[dma((lanes,))] * 6,
            *[dma((ITERS, lanes))] * 2,
            *[dma((ITERS, steps, CHUNKS))] * 4,
            *[dma((ITERS, steps))] * 2,
            *[dma((ITERS, steps, CHUNKS))] * 2,
            *[dma((ITERS, lanes))] * 2,
        ],
        compiler_params=pltpu.CompilerParams(
            collective_id=0, has_side_effects=True, vmem_limit_bytes=63 * 1024 * 1024
        ),
        cost_estimate=pl.CostEstimate(
            flops=ITERS * 18 * block * block * width, bytes_accessed=4 * block * block, transcendentals=0
        ),
    )(embeddings, co_engagement, confidence, tile_offset)


def solution(mesh):
    in_specs = (
        P(("wide", "narrow"), None),
        P("wide", "narrow"),
        P("wide", "narrow"),
        P("wide", "narrow"),
    )
    out_specs = P(("wide", "narrow"), None)
    return jax.shard_map(body, mesh=mesh, in_specs=in_specs, out_specs=out_specs, check_vma=False)
```

```python
import functools
import math

import jax
import jax.numpy as jnp
from jax import lax
from jax.experimental import pallas as pl
from jax.experimental.pallas import tpu as pltpu
from jax.sharding import PartitionSpec as P

ITERS = 2
CHUNKS = 1
HOP = {1: 1, 2: 2, 3: 1, 4: 2}
MESH = pl.DeviceIdType.MESH
F32, BF16 = jnp.float32, jnp.bfloat16
NT = (((1,), (1,)), ((), ()))
TN = (((0,), (0,)), ((), ()))
NN = (((1,), (0,)), ((), ()))


def halves(a):
    hi = a.astype(BF16)
    return hi, (a - hi.astype(F32)).astype(BF16)


def dot3(a_hi, a_lo, b_hi, b_lo, dims):
    dot = functools.partial(lax.dot_general, dimension_numbers=dims, preferred_element_type=F32)
    return dot(a_hi, b_hi) + (dot(a_hi, b_lo) + dot(a_lo, b_hi))


def kernel(
    lanes, wides, rate,
    emb_ref, x_ref, c_ref, off_ref, out_ref,
    off_v, xs, cs, xr, cr, ew, near, ew_hi, ew_lo, f_hi, f_lo, w_hi, w_lo,
    back, sib_part, total, arrived, row_part, row_got, x_in, c_in, pred,
    in_s, off_s, off_r, x_s, x_r, c_s, c_r, ag_s, ag_r, ch_s, ch_r, sb_s, sb_r,
    bs_s, bs_r, bc_s, bc_r, rs_s, rs_r,
):
    rows, width = emb_ref.shape
    block = rows * lanes
    steps = lanes // 2
    part = rows // CHUNKS
    w = lax.axis_index("wide")
    k = lax.axis_index("narrow")
    core = lax.rem(w, 2)
    below = {g: lax.rem(w + wides - 2 * g, wides) for g in (1, 2)}
    above = {g: lax.rem(w + 2 * g, wides) for g in (1, 2)}
    sibling = w + 1 - 2 * core

    def peer(r):
        return lax.rem(k + r, lanes)

    def copy(src, dst, send, recv, wide, narrow):
        return pltpu.make_async_remote_copy(
            src_ref=src, dst_ref=dst, send_sem=send, recv_sem=recv,
            device_id=(wide, narrow), device_id_type=MESH,
        )

    def over_peers(fn):
        def step(r, carry):
            fn(peer(r))
            return carry
        lax.fori_loop(1, lanes, step, 0)

    e_load = pltpu.make_async_copy(emb_ref, near.at[0, 0], in_s.at[0])
    x_load = pltpu.make_async_copy(x_ref, x_in, in_s.at[1])
    c_load = pltpu.make_async_copy(c_ref, c_in, in_s.at[2])
    barrier = pltpu.get_barrier_semaphore()
    over_peers(lambda m: pl.semaphore_signal(barrier, inc=1, device_id=(w, m), device_id_type=MESH))
    for other in (*below.values(), *above.values(), sibling):
        pl.semaphore_signal(barrier, inc=1, device_id=(other, k), device_id_type=MESH)
    e_load.start()
    x_load.start()
    c_load.start()
    off_v[k] = jnp.full(off_v.shape[1:], off_ref[0, 0], jnp.int32)
    for it in range(ITERS):
        sib_part[it, steps * core] = jnp.zeros((rows, width), F32)
    e_load.wait()
    pl.semaphore_wait(barrier, lanes + 4)

    def rows_of(q):
        return pl.ds(q * part, part)

    def gather(it, i, m, piece):
        src = near.at[it, 0] if i < lanes // 2 else ew.at[it, piece]
        return copy(src, ew.at[it, piece], ag_s.at[it, i], ag_r.at[it, piece], w, m)

    neighbour = k + 1 - 2 * lax.rem(k, 2)

    def pass_on(it):
        gather(it, 0, neighbour, neighbour).wait_recv()
        for i in range(1, lanes // 2):
            gather(it, lanes // 2 - 1 + i, peer(2 * i), neighbour).start()

    def down(it, h, q):
        return copy(
            near.at[it, 2 * (h - HOP[h]), rows_of(q)], near.at[it, 2 * h, rows_of(q)],
            ch_s.at[it, h - 1, q], ch_r.at[it, h - 1, q], below[HOP[h]], k,
        )

    def to_sibling(it, t, q):
        return copy(
            near.at[it, 2 * t + 2 - 2 * core, rows_of(q)], near.at[it, 2 * t + 1, rows_of(q)],
            sb_s.at[it, t, q], sb_r.at[it, t, q], sibling, k,
        )

    def offsets(m, slot):
        return copy(off_v.at[k], off_v.at[slot], off_s.at[m], off_r.at[slot], w, m)

    def x_copy(m, slot):
        return copy(xs.at[m], xr.at[slot], x_s.at[m], x_r.at[slot], w, m)

    def c_copy(m, slot):
        return copy(cs.at[m], cr.at[slot], c_s.at[m], c_r.at[slot], w, m)

    def back_sibling(it, t):
        return copy(
            back.at[it, 2 * t], sib_part.at[it, t + core], bs_s.at[it, t], bs_r.at[it, t], sibling, k
        )

    def up(it, h, q):
        return copy(
            total.at[it, h - 1, rows_of(q)], arrived.at[it, h - 1, rows_of(q)],
            bc_s.at[it, h - 1, q], bc_r.at[it, h - 1, q], above[HOP[h]], k,
        )

    def scatter(it, m, slot):
        return copy(row_part.at[it, m], row_got.at[it, slot], rs_s.at[it, m], rs_r.at[it, slot], w, m)

    def start_forward(it):
        for h in (2, 1):
            for q in range(CHUNKS):
                down(it, h, q).start()

        @pl.when(core == 1)
        def _():
            for q in range(CHUNKS):
                to_sibling(it, 0, q).start()

        for i in range(lanes // 2):
            gather(it, i, peer(2 * i) if i else neighbour, k).start()
        ew[it, k] = near[it, 0]

    def forward(it, u):
        for q in range(CHUNKS):
            down(it, u, q).wait_recv()
            if u == 2:
                down(it, 4, q).start()
                down(it, 3, q).start()
            if u < steps:
                to_sibling(it, u - 1 + core, q).start()
            else:
                @pl.when(core == 0)
                def _():
                    to_sibling(it, steps - 1, q).start()

    def wait_gather(it):
        over_peers(
            lambda m: pl.when(m != neighbour)(lambda: gather(it, 1, m, m).wait_recv())
        )
        hi, lo = halves(ew[it].reshape(block, width))
        ew_hi[...] = hi
        ew_lo[...] = lo

    def predict(it, first, last):
        for t in range(first - 1, last):
            for q in range(CHUNKS):
                to_sibling(it, t, q).wait_recv()
        some = pl.ds((2 * first - 2) * rows, 2 * (last - first + 1) * rows)
        fh, fl = halves(near[it, 2 * first - 1:2 * last + 1].reshape(some.size, width))
        f_hi[some] = fh
        f_lo[some] = fl
        pred[some] = dot3(fh, fl, ew_hi[...], ew_lo[...], NT)

    def tile(it, first, last, slot_of):
        some = pl.ds((2 * first - 2) * rows, 2 * (last - first + 1) * rows)
        for d in range(2 * first - 2, 2 * last):
            here = pl.ds(d * rows, rows)
            wh, wl = halves(cr[slot_of[d]] * (xr[slot_of[d]] - pred[here]))
            w_hi[here] = wh
            w_lo[here] = wl
        out = dot3(w_hi[some], w_lo[some], ew_hi[...], ew_lo[...], NN)
        back[it, 2 * first - 2:2 * last] = out.reshape(2 * (last - first + 1), rows, width)
        for u in range(first, last + 1):
            back_sibling(it, u - 1).start()

    def wait_sibling_part(it, u):
        if u == steps:
            @pl.when(core == 0)
            def _():
                back_sibling(it, steps - 1).wait_recv()
        elif u == 0:
            @pl.when(core == 1)
            def _():
                back_sibling(it, 0).wait_recv()
        else:
            back_sibling(it, u - 1 + core).wait_recv()

    def backward(it, h):
        wait_sibling_part(it, h)
        for q in range(CHUNKS):
            here = rows_of(q)
            value = back[it, 2 * h - 1, here] + sib_part[it, h, here]
            if h == 2:
                for far in (3, 4):
                    up(it, far, q).wait_recv()
                    value = value + arrived[it, far - 1, here]
            total[it, h - 1, here] = value
            up(it, h, q).start()

    def row_terms(it):
        terms = dot3(w_hi[...], w_lo[...], f_hi[...], f_lo[...], TN)
        row_part[it] = terms.reshape(lanes, rows, width)
        row_got[it, k] = row_part[it, k]
        over_peers(lambda m: scatter(it, m, k).start())

    def finish(it, store):
        over_peers(lambda m: scatter(it, m, m).wait_recv())
        wait_sibling_part(it, 0)
        grad = row_got[it, 0] + sib_part[it, 0]
        for m in range(1, lanes):
            grad = grad + row_got[it, m]
        for q in range(CHUNKS):
            here = rows_of(q)
            terms = grad[q * part:(q + 1) * part]
            for h in (1, 2):
                up(it, h, q).wait_recv()
                terms = terms + arrived[it, h - 1, here]
            store(here, near[it, 0, here] + rate * terms)

    def keep(here, value):
        near[1, 0, here] = value

    def result(here, value):
        out_ref[here] = value

    start_forward(0)
    over_peers(lambda m: offsets(m, k).start())

    def transpose(ref, out):
        eye = (
            lax.broadcasted_iota(jnp.int32, (block, block), 0)
            == lax.broadcasted_iota(jnp.int32, (block, block), 1)
        )
        eye = jnp.where(eye, 1.0, 0.0).astype(BF16)
        out[...] = lax.dot_general(eye, ref[...], NT, preferred_element_type=F32).reshape(out.shape)

    x_load.wait()
    transpose(x_in, xs)
    over_peers(lambda m: x_copy(m, k).start())
    c_load.wait()
    transpose(c_in, cs)
    pass_on(0)
    over_peers(lambda m: c_copy(m, k).start())
    xr[k] = xs[k]
    cr[k] = cs[k]

    for it in range(ITERS):
        if it == 0:
            for u in (2, 1, 3, 4):
                forward(it, u)
            wait_gather(it)
            predict(it, 1, steps)
            over_peers(lambda m: offsets(m, m).wait_recv())
            offs = [jnp.max(off_v[s]) for s in range(lanes)]
            slot_of = []
            for d in range(lanes):
                found = jnp.int32(0)
                for s in range(1, lanes):
                    found = jnp.where(offs[s] == d, s, found)
                slot_of.append(found)
            over_peers(lambda m: x_copy(m, m).wait_recv())
            over_peers(lambda m: c_copy(m, m).wait_recv())
            tile(it, steps, steps, slot_of)
            tile(it, 1, steps - 1, slot_of)
        else:
            pass_on(it)
            forward(it, 2)
            forward(it, 1)
            wait_gather(it)
            predict(it, 1, 2)
            tile(it, 1, 2, slot_of)
            forward(it, 3)
            forward(it, 4)
            predict(it, 3, 4)
            tile(it, 3, 4, slot_of)
        row_terms(it)
        backward(it, 4)
        backward(it, 3)
        backward(it, 1)
        backward(it, 2)
        finish(it, keep if it < ITERS - 1 else result)
        if it < ITERS - 1:
            start_forward(it + 1)

    def drain(m):
        offsets(m, k).wait_send()
        x_copy(m, k).wait_send()
        c_copy(m, k).wait_send()
        for it in range(ITERS):
            scatter(it, m, k).wait_send()

    over_peers(drain)
    for it in range(ITERS):
        for i in range(lanes - 1):
            gather(it, i, neighbour, k if i < lanes // 2 else neighbour).wait_send()
        for t in range(steps):
            back_sibling(it, t).wait_send()
            for q in range(CHUNKS):
                down(it, t + 1, q).wait_send()
                to_sibling(it, t, q).wait_send()
                up(it, t + 1, q).wait_send()


def body(embeddings, co_engagement, confidence, tile_offset):
    rows, width = embeddings.shape
    lanes = lax.axis_size("narrow")
    wides = lax.axis_size("wide")
    block = rows * lanes
    steps = lanes // 2
    rate = 0.75 * math.sqrt(width) / (lanes * block)
    vmem = pl.BlockSpec(memory_space=pltpu.VMEM)
    hbm = pl.BlockSpec(memory_space=pltpu.HBM)
    dma = pltpu.SemaphoreType.DMA
    return pl.pallas_call(
        functools.partial(kernel, lanes, wides, rate),
        out_shape=jax.ShapeDtypeStruct((rows, width), F32),
        in_specs=[hbm, hbm, hbm, pl.BlockSpec(memory_space=pltpu.SMEM)],
        out_specs=vmem,
        scratch_shapes=[
            pltpu.VMEM((lanes, 8, 128), jnp.int32),
            *[pltpu.VMEM((lanes, rows, block), F32)] * 4,
            pltpu.VMEM((ITERS, lanes, rows, width), F32),
            pltpu.VMEM((ITERS, lanes + 1, rows, width), F32),
            *[pltpu.VMEM((block, width), BF16)] * 4,
            *[pltpu.VMEM((block, block), BF16)] * 2,
            pltpu.VMEM((ITERS, lanes, rows, width), F32),
            pltpu.VMEM((ITERS, steps + 1, rows, width), F32),
            pltpu.VMEM((ITERS, steps, rows, width), F32),
            pltpu.VMEM((ITERS, steps, rows, width), F32),
            pltpu.VMEM((ITERS, lanes, rows, width), F32),
            pltpu.VMEM((ITERS, lanes, rows, width), F32),
            *[pltpu.VMEM((block, block), BF16)] * 2,
            pltpu.VMEM((block, block), F32),
            dma((3,)),
            *[dma((lanes,))] * 6,
            *[dma((ITERS, lanes))] * 2,
            *[dma((ITERS, steps, CHUNKS))] * 4,
            *[dma((ITERS, steps))] * 2,
            *[dma((ITERS, steps, CHUNKS))] * 2,
            *[dma((ITERS, lanes))] * 2,
        ],
        compiler_params=pltpu.CompilerParams(
            collective_id=0, has_side_effects=True, vmem_limit_bytes=54784 * 1024
        ),
        cost_estimate=pl.CostEstimate(
            flops=ITERS * 18 * block * block * width, bytes_accessed=4 * block * block, transcendentals=0
        ),
    )(embeddings, co_engagement, confidence, tile_offset)


def solution(mesh):
    in_specs = (
        P(("wide", "narrow"), None),
        P("wide", "narrow"),
        P("wide", "narrow"),
        P("wide", "narrow"),
    )
    out_specs = P(("wide", "narrow"), None)
    return jax.shard_map(body, mesh=mesh, in_specs=in_specs, out_specs=out_specs, check_vma=False)
```

```python
import functools
import math

import jax
import jax.numpy as jnp
from jax import lax
from jax.experimental import pallas as pl
from jax.experimental.pallas import tpu as pltpu
from jax.sharding import PartitionSpec as P

ITERS = 2
CHUNKS = 1
HOP = {1: 1, 2: 2, 3: 1, 4: 2}
MESH = pl.DeviceIdType.MESH
F32, BF16 = jnp.float32, jnp.bfloat16
NT = (((1,), (1,)), ((), ()))
TN = (((0,), (0,)), ((), ()))
NN = (((1,), (0,)), ((), ()))


def halves(a):
    hi = a.astype(BF16)
    return hi, (a - hi.astype(F32)).astype(BF16)


def dot3(a_hi, a_lo, b_hi, b_lo, dims):
    dot = functools.partial(lax.dot_general, dimension_numbers=dims, preferred_element_type=F32)
    return dot(a_hi, b_hi) + (dot(a_hi, b_lo) + dot(a_lo, b_hi))


def kernel(
    lanes, wides, rate,
    emb_ref, x_ref, c_ref, off_ref, out_ref,
    off_v, xs, cs, xr, cr, ew, near, ew_hi, ew_lo, f_hi, f_lo, w_hi, w_lo,
    back, sib_part, total, arrived, row_part, row_got, x_in, c_in, pred,
    in_s, off_s, off_r, x_s, x_r, c_s, c_r, ag_s, ag_r, ch_s, ch_r, sb_s, sb_r,
    bs_s, bs_r, bc_s, bc_r, rs_s, rs_r,
):
    rows, width = emb_ref.shape
    block = rows * lanes
    steps = lanes // 2
    part = rows // CHUNKS
    w = lax.axis_index("wide")
    k = lax.axis_index("narrow")
    core = lax.rem(w, 2)
    below = {g: lax.rem(w + wides - 2 * g, wides) for g in (1, 2)}
    above = {g: lax.rem(w + 2 * g, wides) for g in (1, 2)}
    sibling = w + 1 - 2 * core

    def peer(r):
        return lax.rem(k + r, lanes)

    def copy(src, dst, send, recv, wide, narrow):
        return pltpu.make_async_remote_copy(
            src_ref=src, dst_ref=dst, send_sem=send, recv_sem=recv,
            device_id=(wide, narrow), device_id_type=MESH,
        )

    def over_peers(fn):
        def step(r, carry):
            fn(peer(r))
            return carry
        lax.fori_loop(1, lanes, step, 0)

    e_load = pltpu.make_async_copy(emb_ref, near.at[0, 0], in_s.at[0])
    x_load = pltpu.make_async_copy(x_ref, x_in, in_s.at[1])
    c_load = pltpu.make_async_copy(c_ref, c_in, in_s.at[2])
    barrier = pltpu.get_barrier_semaphore()
    over_peers(lambda m: pl.semaphore_signal(barrier, inc=1, device_id=(w, m), device_id_type=MESH))
    for other in (*below.values(), *above.values(), sibling):
        pl.semaphore_signal(barrier, inc=1, device_id=(other, k), device_id_type=MESH)
    e_load.start()
    x_load.start()
    c_load.start()
    off_v[k] = jnp.full(off_v.shape[1:], off_ref[0, 0], jnp.int32)
    for it in range(ITERS):
        sib_part[it, steps * core] = jnp.zeros((rows, width), F32)
    e_load.wait()
    pl.semaphore_wait(barrier, lanes + 4)

    def rows_of(q):
        return pl.ds(q * part, part)

    def gather(it, i, m, piece):
        src = near.at[it, 0] if i < lanes // 2 else ew.at[it, piece]
        return copy(src, ew.at[it, piece], ag_s.at[it, i], ag_r.at[it, piece], w, m)

    def direct(it, m, piece):
        return copy(near.at[it, 0], ew.at[it, piece], ag_s.at[it, m], ag_r.at[it, piece], w, m)

    neighbour = k + 1 - 2 * lax.rem(k, 2)

    def pass_on(it):
        gather(it, 0, neighbour, neighbour).wait_recv()
        for i in range(1, lanes // 2):
            gather(it, lanes // 2 - 1 + i, peer(2 * i), neighbour).start()

    def down(it, h, q):
        return copy(
            near.at[it, 2 * (h - HOP[h]), rows_of(q)], near.at[it, 2 * h, rows_of(q)],
            ch_s.at[it, h - 1, q], ch_r.at[it, h - 1, q], below[HOP[h]], k,
        )

    def to_sibling(it, t, q):
        return copy(
            near.at[it, 2 * t + 2 - 2 * core, rows_of(q)], near.at[it, 2 * t + 1, rows_of(q)],
            sb_s.at[it, t, q], sb_r.at[it, t, q], sibling, k,
        )

    def offsets(m, slot):
        return copy(off_v.at[k], off_v.at[slot], off_s.at[m], off_r.at[slot], w, m)

    def x_copy(m, slot):
        return copy(xs.at[m], xr.at[slot], x_s.at[m], x_r.at[slot], w, m)

    def c_copy(m, slot):
        return copy(cs.at[m], cr.at[slot], c_s.at[m], c_r.at[slot], w, m)

    def back_sibling(it, t):
        return copy(
            back.at[it, 2 * t], sib_part.at[it, t + core], bs_s.at[it, t], bs_r.at[it, t], sibling, k
        )

    def up(it, h, q):
        return copy(
            total.at[it, h - 1, rows_of(q)], arrived.at[it, h - 1, rows_of(q)],
            bc_s.at[it, h - 1, q], bc_r.at[it, h - 1, q], above[HOP[h]], k,
        )

    def scatter(it, m, slot):
        return copy(row_part.at[it, m], row_got.at[it, slot], rs_s.at[it, m], rs_r.at[it, slot], w, m)

    def start_forward(it):
        for h in (2, 1):
            for q in range(CHUNKS):
                down(it, h, q).start()

        @pl.when(core == 1)
        def _():
            for q in range(CHUNKS):
                to_sibling(it, 0, q).start()

        if it == 0:
            for i in range(lanes // 2):
                gather(it, i, peer(2 * i) if i else neighbour, k).start()
        else:
            over_peers(lambda m: direct(it, m, k).start())
        ew[it, k] = near[it, 0]

    def forward(it, u):
        for q in range(CHUNKS):
            down(it, u, q).wait_recv()
            if u == 2:
                down(it, 4, q).start()
                down(it, 3, q).start()
            if u < steps:
                to_sibling(it, u - 1 + core, q).start()
            else:
                @pl.when(core == 0)
                def _():
                    to_sibling(it, steps - 1, q).start()

    def wait_gather(it):
        if it == 0:
            over_peers(
                lambda m: pl.when(m != neighbour)(lambda: gather(it, 1, m, m).wait_recv())
            )
        else:
            over_peers(lambda m: direct(it, m, m).wait_recv())
        hi, lo = halves(ew[it].reshape(block, width))
        ew_hi[...] = hi
        ew_lo[...] = lo

    def predict(it, first, last):
        for t in range(first - 1, last):
            for q in range(CHUNKS):
                to_sibling(it, t, q).wait_recv()
        some = pl.ds((2 * first - 2) * rows, 2 * (last - first + 1) * rows)
        fh, fl = halves(near[it, 2 * first - 1:2 * last + 1].reshape(some.size, width))
        f_hi[some] = fh
        f_lo[some] = fl
        pred[some] = dot3(fh, fl, ew_hi[...], ew_lo[...], NT)

    def tile(it, first, last, slot_of):
        some = pl.ds((2 * first - 2) * rows, 2 * (last - first + 1) * rows)
        for d in range(2 * first - 2, 2 * last):
            here = pl.ds(d * rows, rows)
            wh, wl = halves(cr[slot_of[d]] * (xr[slot_of[d]] - pred[here]))
            w_hi[here] = wh
            w_lo[here] = wl
        out = dot3(w_hi[some], w_lo[some], ew_hi[...], ew_lo[...], NN)
        back[it, 2 * first - 2:2 * last] = out.reshape(2 * (last - first + 1), rows, width)
        for u in range(last, first - 1, -1):
            back_sibling(it, u - 1).start()

    def wait_sibling_part(it, u):
        if u == steps:
            @pl.when(core == 0)
            def _():
                back_sibling(it, steps - 1).wait_recv()
        elif u == 0:
            @pl.when(core == 1)
            def _():
                back_sibling(it, 0).wait_recv()
        else:
            back_sibling(it, u - 1 + core).wait_recv()

    def backward(it, h):
        wait_sibling_part(it, h)
        for q in range(CHUNKS):
            here = rows_of(q)
            value = back[it, 2 * h - 1, here] + sib_part[it, h, here]
            if h == 2:
                for far in (3, 4):
                    up(it, far, q).wait_recv()
                    value = value + arrived[it, far - 1, here]
            total[it, h - 1, here] = value
            up(it, h, q).start()

    def row_terms(it):
        terms = dot3(w_hi[...], w_lo[...], f_hi[...], f_lo[...], TN)
        row_part[it] = terms.reshape(lanes, rows, width)
        row_got[it, k] = row_part[it, k]
        over_peers(lambda m: scatter(it, m, k).start())

    def finish(it, store):
        over_peers(lambda m: scatter(it, m, m).wait_recv())
        wait_sibling_part(it, 0)
        grad = row_got[it, 0] + sib_part[it, 0]
        for m in range(1, lanes):
            grad = grad + row_got[it, m]
        for q in range(CHUNKS):
            here = rows_of(q)
            terms = grad[q * part:(q + 1) * part]
            for h in (1, 2):
                up(it, h, q).wait_recv()
                terms = terms + arrived[it, h - 1, here]
            store(here, near[it, 0, here] + rate * terms)

    def keep(here, value):
        near[1, 0, here] = value

    def result(here, value):
        out_ref[here] = value

    start_forward(0)
    over_peers(lambda m: offsets(m, k).start())

    def transpose(ref, out):
        eye = (
            lax.broadcasted_iota(jnp.int32, (block, block), 0)
            == lax.broadcasted_iota(jnp.int32, (block, block), 1)
        )
        eye = jnp.where(eye, 1.0, 0.0).astype(BF16)
        out[...] = lax.dot_general(eye, ref[...], NT, preferred_element_type=F32).reshape(out.shape)

    x_load.wait()
    transpose(x_in, xs)
    over_peers(lambda m: x_copy(m, k).start())
    c_load.wait()
    transpose(c_in, cs)
    pass_on(0)
    over_peers(lambda m: c_copy(m, k).start())
    xr[k] = xs[k]
    cr[k] = cs[k]

    for it in range(ITERS):
        if it == 0:
            for u in (2, 1, 3, 4):
                forward(it, u)
            wait_gather(it)
            predict(it, 1, steps)
            over_peers(lambda m: offsets(m, m).wait_recv())
            offs = [jnp.max(off_v[s]) for s in range(lanes)]
            slot_of = []
            for d in range(lanes):
                found = jnp.int32(0)
                for s in range(1, lanes):
                    found = jnp.where(offs[s] == d, s, found)
                slot_of.append(found)
            over_peers(lambda m: x_copy(m, m).wait_recv())
            over_peers(lambda m: c_copy(m, m).wait_recv())
            tile(it, steps, steps, slot_of)
            tile(it, 1, steps - 1, slot_of)
        else:
            forward(it, 2)
            forward(it, 1)
            wait_gather(it)
            predict(it, 1, 2)
            tile(it, 1, 2, slot_of)
            forward(it, 3)
            forward(it, 4)
            predict(it, 3, 4)
            tile(it, 3, 4, slot_of)
        row_terms(it)
        backward(it, 4)
        backward(it, 3)
        backward(it, 1)
        backward(it, 2)
        finish(it, keep if it < ITERS - 1 else result)
        if it < ITERS - 1:
            start_forward(it + 1)

    def drain(m):
        offsets(m, k).wait_send()
        x_copy(m, k).wait_send()
        c_copy(m, k).wait_send()
        for it in range(ITERS):
            scatter(it, m, k).wait_send()

    over_peers(drain)
    for it in range(ITERS):
        if it == 0:
            for i in range(lanes - 1):
                gather(it, i, neighbour, k if i < lanes // 2 else neighbour).wait_send()
        else:
            over_peers(lambda m: direct(it, m, k).wait_send())
        for t in range(steps):
            back_sibling(it, t).wait_send()
            for q in range(CHUNKS):
                down(it, t + 1, q).wait_send()
                to_sibling(it, t, q).wait_send()
                up(it, t + 1, q).wait_send()


def body(embeddings, co_engagement, confidence, tile_offset):
    rows, width = embeddings.shape
    lanes = lax.axis_size("narrow")
    wides = lax.axis_size("wide")
    block = rows * lanes
    steps = lanes // 2
    rate = 0.75 * math.sqrt(width) / (lanes * block)
    vmem = pl.BlockSpec(memory_space=pltpu.VMEM)
    hbm = pl.BlockSpec(memory_space=pltpu.HBM)
    dma = pltpu.SemaphoreType.DMA
    return pl.pallas_call(
        functools.partial(kernel, lanes, wides, rate),
        out_shape=jax.ShapeDtypeStruct((rows, width), F32),
        in_specs=[hbm, hbm, hbm, pl.BlockSpec(memory_space=pltpu.SMEM)],
        out_specs=vmem,
        scratch_shapes=[
            pltpu.VMEM((lanes, 8, 128), jnp.int32),
            *[pltpu.VMEM((lanes, rows, block), F32)] * 4,
            pltpu.VMEM((ITERS, lanes, rows, width), F32),
            pltpu.VMEM((ITERS, lanes + 1, rows, width), F32),
            *[pltpu.VMEM((block, width), BF16)] * 4,
            *[pltpu.VMEM((block, block), BF16)] * 2,
            pltpu.VMEM((ITERS, lanes, rows, width), F32),
            pltpu.VMEM((ITERS, steps + 1, rows, width), F32),
            pltpu.VMEM((ITERS, steps, rows, width), F32),
            pltpu.VMEM((ITERS, steps, rows, width), F32),
            pltpu.VMEM((ITERS, lanes, rows, width), F32),
            pltpu.VMEM((ITERS, lanes, rows, width), F32),
            *[pltpu.VMEM((block, block), BF16)] * 2,
            pltpu.VMEM((block, block), F32),
            dma((3,)),
            *[dma((lanes,))] * 6,
            *[dma((ITERS, lanes))] * 2,
            *[dma((ITERS, steps, CHUNKS))] * 4,
            *[dma((ITERS, steps))] * 2,
            *[dma((ITERS, steps, CHUNKS))] * 2,
            *[dma((ITERS, lanes))] * 2,
        ],
        compiler_params=pltpu.CompilerParams(
            collective_id=0, has_side_effects=True, vmem_limit_bytes=54784 * 1024
        ),
        cost_estimate=pl.CostEstimate(
            flops=ITERS * 18 * block * block * width, bytes_accessed=4 * block * block, transcendentals=0
        ),
    )(embeddings, co_engagement, confidence, tile_offset)


def solution(mesh):
    in_specs = (
        P(("wide", "narrow"), None),
        P("wide", "narrow"),
        P("wide", "narrow"),
        P("wide", "narrow"),
    )
    out_specs = P(("wide", "narrow"), None)
    return jax.shard_map(body, mesh=mesh, in_specs=in_specs, out_specs=out_specs, check_vma=False)
```

```python
import functools
import math

import jax
import jax.numpy as jnp
from jax import lax
from jax.experimental import pallas as pl
from jax.experimental.pallas import tpu as pltpu
from jax.sharding import PartitionSpec as P

ITERS = 2
CHUNKS = 1
HOP = {1: 1, 2: 2, 3: 1, 4: 2}
MESH = pl.DeviceIdType.MESH
F32, BF16 = jnp.float32, jnp.bfloat16
NT = (((1,), (1,)), ((), ()))
TN = (((0,), (0,)), ((), ()))
NN = (((1,), (0,)), ((), ()))


def halves(a):
    hi = a.astype(BF16)
    return hi, (a - hi.astype(F32)).astype(BF16)


def dot3(a_hi, a_lo, b_hi, b_lo, dims):
    dot = functools.partial(lax.dot_general, dimension_numbers=dims, preferred_element_type=F32)
    return dot(a_hi, b_hi) + (dot(a_hi, b_lo) + dot(a_lo, b_hi))


def kernel(
    lanes, wides, rate,
    emb_ref, x_ref, c_ref, off_ref, out_ref,
    off_v, xs, cs, xr, cr, ew, near, ew_hi, ew_lo, f_hi, f_lo, w_hi, w_lo,
    back, sib_part, total, arrived, row_part, row_got, x_in, c_in, pred,
    in_s, off_s, off_r, x_s, x_r, c_s, c_r, ag_s, ag_r, ch_s, ch_r, sb_s, sb_r,
    bs_s, bs_r, bc_s, bc_r, rs_s, rs_r,
):
    rows, width = emb_ref.shape
    block = rows * lanes
    steps = lanes // 2
    part = rows // CHUNKS
    w = lax.axis_index("wide")
    k = lax.axis_index("narrow")
    core = lax.rem(w, 2)
    below = {g: lax.rem(w + wides - 2 * g, wides) for g in (1, 2)}
    above = {g: lax.rem(w + 2 * g, wides) for g in (1, 2)}
    sibling = w + 1 - 2 * core

    def peer(r):
        return lax.rem(k + r, lanes)

    def copy(src, dst, send, recv, wide, narrow):
        return pltpu.make_async_remote_copy(
            src_ref=src, dst_ref=dst, send_sem=send, recv_sem=recv,
            device_id=(wide, narrow), device_id_type=MESH,
        )

    def over_peers(fn):
        def step(r, carry):
            fn(peer(r))
            return carry
        lax.fori_loop(1, lanes, step, 0)

    e_load = pltpu.make_async_copy(emb_ref, near.at[0, 0], in_s.at[0])
    x_load = pltpu.make_async_copy(x_ref, x_in, in_s.at[1])
    c_load = pltpu.make_async_copy(c_ref, c_in, in_s.at[2])
    barrier = pltpu.get_barrier_semaphore()
    over_peers(lambda m: pl.semaphore_signal(barrier, inc=1, device_id=(w, m), device_id_type=MESH))
    for other in (*below.values(), *above.values(), sibling):
        pl.semaphore_signal(barrier, inc=1, device_id=(other, k), device_id_type=MESH)
    e_load.start()
    x_load.start()
    c_load.start()
    off_v[k] = jnp.full(off_v.shape[1:], off_ref[0, 0], jnp.int32)
    for it in range(ITERS):
        sib_part[it, steps * core] = jnp.zeros((rows, width), F32)
    e_load.wait()
    pl.semaphore_wait(barrier, lanes + 4)

    def rows_of(q):
        return pl.ds(q * part, part)

    def gather(it, i, m, piece):
        src = near.at[it, 0] if i < lanes // 2 else ew.at[it, piece]
        return copy(src, ew.at[it, piece], ag_s.at[it, i], ag_r.at[it, piece], w, m)

    def direct(it, m, piece):
        return copy(near.at[it, 0], ew.at[it, piece], ag_s.at[it, m], ag_r.at[it, piece], w, m)

    neighbour = k + 1 - 2 * lax.rem(k, 2)

    def pass_on(it):
        gather(it, 0, neighbour, neighbour).wait_recv()
        for i in range(1, lanes // 2):
            gather(it, lanes // 2 - 1 + i, peer(2 * i), neighbour).start()

    def down(it, h, q):
        return copy(
            near.at[it, 2 * (h - HOP[h]), rows_of(q)], near.at[it, 2 * h, rows_of(q)],
            ch_s.at[it, h - 1, q], ch_r.at[it, h - 1, q], below[HOP[h]], k,
        )

    def to_sibling(it, t, q):
        return copy(
            near.at[it, 2 * t + 2 - 2 * core, rows_of(q)], near.at[it, 2 * t + 1, rows_of(q)],
            sb_s.at[it, t, q], sb_r.at[it, t, q], sibling, k,
        )

    def offsets(m, slot):
        return copy(off_v.at[k], off_v.at[slot], off_s.at[m], off_r.at[slot], w, m)

    def x_copy(m, slot):
        return copy(xs.at[m], xr.at[slot], x_s.at[m], x_r.at[slot], w, m)

    def c_copy(m, slot):
        return copy(cs.at[m], cr.at[slot], c_s.at[m], c_r.at[slot], w, m)

    def back_sibling(it, t):
        return copy(
            back.at[it, 2 * t], sib_part.at[it, t + core], bs_s.at[it, t], bs_r.at[it, t], sibling, k
        )

    def up(it, h, q):
        return copy(
            total.at[it, h - 1, rows_of(q)], arrived.at[it, h - 1, rows_of(q)],
            bc_s.at[it, h - 1, q], bc_r.at[it, h - 1, q], above[HOP[h]], k,
        )

    def scatter(it, m, slot):
        return copy(row_part.at[it, m], row_got.at[it, slot], rs_s.at[it, m], rs_r.at[it, slot], w, m)

    def start_forward(it):
        for h in (2, 1):
            for q in range(CHUNKS):
                down(it, h, q).start()

        @pl.when(core == 1)
        def _():
            for q in range(CHUNKS):
                to_sibling(it, 0, q).start()

        if it == 0:
            for i in range(lanes // 2):
                gather(it, i, peer(2 * i) if i else neighbour, k).start()
        else:
            over_peers(lambda m: direct(it, m, k).start())
        ew[it, k] = near[it, 0]

    def forward(it, u):
        for q in range(CHUNKS):
            down(it, u, q).wait_recv()
            if u == 2:
                down(it, 4, q).start()
                down(it, 3, q).start()
            if u < steps:
                to_sibling(it, u - 1 + core, q).start()
            else:
                @pl.when(core == 0)
                def _():
                    to_sibling(it, steps - 1, q).start()

    def wait_gather(it):
        if it == 0:
            over_peers(
                lambda m: pl.when(m != neighbour)(lambda: gather(it, 1, m, m).wait_recv())
            )
        else:
            over_peers(lambda m: direct(it, m, m).wait_recv())
        hi, lo = halves(ew[it].reshape(block, width))
        ew_hi[...] = hi
        ew_lo[...] = lo

    def predict(it, first, last):
        for t in range(first - 1, last):
            for q in range(CHUNKS):
                to_sibling(it, t, q).wait_recv()
        some = pl.ds((2 * first - 2) * rows, 2 * (last - first + 1) * rows)
        fh, fl = halves(near[it, 2 * first - 1:2 * last + 1].reshape(some.size, width))
        f_hi[some] = fh
        f_lo[some] = fl
        pred[some] = dot3(fh, fl, ew_hi[...], ew_lo[...], NT)

    def tile(it, first, last, slot_of):
        some = pl.ds((2 * first - 2) * rows, 2 * (last - first + 1) * rows)
        for d in range(2 * first - 2, 2 * last):
            here = pl.ds(d * rows, rows)
            wh, wl = halves(cr[slot_of[d]] * (xr[slot_of[d]] - pred[here]))
            w_hi[here] = wh
            w_lo[here] = wl
        out = dot3(w_hi[some], w_lo[some], ew_hi[...], ew_lo[...], NN)
        back[it, 2 * first - 2:2 * last] = out.reshape(2 * (last - first + 1), rows, width)
        for u in range(last, first - 1, -1):
            back_sibling(it, u - 1).start()

    def wait_sibling_part(it, u):
        if u == steps:
            @pl.when(core == 0)
            def _():
                back_sibling(it, steps - 1).wait_recv()
        elif u == 0:
            @pl.when(core == 1)
            def _():
                back_sibling(it, 0).wait_recv()
        else:
            back_sibling(it, u - 1 + core).wait_recv()

    def backward(it, h):
        wait_sibling_part(it, h)
        for q in range(CHUNKS):
            here = rows_of(q)
            value = back[it, 2 * h - 1, here] + sib_part[it, h, here]
            if h == 2:
                for far in (3, 4):
                    up(it, far, q).wait_recv()
                    value = value + arrived[it, far - 1, here]
            total[it, h - 1, here] = value
            up(it, h, q).start()

    def row_terms(it):
        terms = dot3(w_hi[...], w_lo[...], f_hi[...], f_lo[...], TN)
        row_part[it] = terms.reshape(lanes, rows, width)
        row_got[it, k] = row_part[it, k]
        over_peers(lambda m: scatter(it, m, k).start())

    def finish(it, store):
        over_peers(lambda m: scatter(it, m, m).wait_recv())
        wait_sibling_part(it, 0)
        grad = row_got[it, 0] + sib_part[it, 0]
        for m in range(1, lanes):
            grad = grad + row_got[it, m]
        for q in range(CHUNKS):
            here = rows_of(q)
            terms = grad[q * part:(q + 1) * part]
            for h in (1, 2):
                up(it, h, q).wait_recv()
                terms = terms + arrived[it, h - 1, here]
            store(here, near[it, 0, here] + rate * terms)

    def keep(here, value):
        near[1, 0, here] = value

    def result(here, value):
        out_ref[here] = value

    start_forward(0)
    over_peers(lambda m: offsets(m, k).start())

    def transpose(ref, out):
        eye = (
            lax.broadcasted_iota(jnp.int32, (block, block), 0)
            == lax.broadcasted_iota(jnp.int32, (block, block), 1)
        )
        eye = jnp.where(eye, 1.0, 0.0).astype(BF16)
        out[...] = lax.dot_general(eye, ref[...], NT, preferred_element_type=F32).reshape(out.shape)

    x_load.wait()
    transpose(x_in, xs)
    over_peers(lambda m: x_copy(m, k).start())
    c_load.wait()
    transpose(c_in, cs)
    pass_on(0)
    over_peers(lambda m: c_copy(m, k).start())
    xr[k] = xs[k]
    cr[k] = cs[k]

    for it in range(ITERS):
        if it == 0:
            for u in (2, 1, 3, 4):
                forward(it, u)
            wait_gather(it)
            predict(it, 1, steps)
            over_peers(lambda m: offsets(m, m).wait_recv())
            offs = [jnp.max(off_v[s]) for s in range(lanes)]
            slot_of = []
            for d in range(lanes):
                found = jnp.int32(0)
                for s in range(1, lanes):
                    found = jnp.where(offs[s] == d, s, found)
                slot_of.append(found)
            over_peers(lambda m: x_copy(m, m).wait_recv())
            over_peers(lambda m: c_copy(m, m).wait_recv())
            tile(it, 1, steps, slot_of)
        else:
            forward(it, 2)
            forward(it, 1)
            wait_gather(it)
            predict(it, 1, 2)
            tile(it, 1, 2, slot_of)
            forward(it, 3)
            forward(it, 4)
            predict(it, 3, 4)
            tile(it, 3, 4, slot_of)
        row_terms(it)
        backward(it, 4)
        backward(it, 3)
        backward(it, 1)
        backward(it, 2)
        finish(it, keep if it < ITERS - 1 else result)
        if it < ITERS - 1:
            start_forward(it + 1)

    def drain(m):
        offsets(m, k).wait_send()
        x_copy(m, k).wait_send()
        c_copy(m, k).wait_send()
        for it in range(ITERS):
            scatter(it, m, k).wait_send()

    over_peers(drain)
    for it in range(ITERS):
        if it == 0:
            for i in range(lanes - 1):
                gather(it, i, neighbour, k if i < lanes // 2 else neighbour).wait_send()
        else:
            over_peers(lambda m: direct(it, m, k).wait_send())
        for t in range(steps):
            back_sibling(it, t).wait_send()
            for q in range(CHUNKS):
                down(it, t + 1, q).wait_send()
                to_sibling(it, t, q).wait_send()
                up(it, t + 1, q).wait_send()


def body(embeddings, co_engagement, confidence, tile_offset):
    rows, width = embeddings.shape
    lanes = lax.axis_size("narrow")
    wides = lax.axis_size("wide")
    block = rows * lanes
    steps = lanes // 2
    rate = 0.75 * math.sqrt(width) / (lanes * block)
    vmem = pl.BlockSpec(memory_space=pltpu.VMEM)
    hbm = pl.BlockSpec(memory_space=pltpu.HBM)
    dma = pltpu.SemaphoreType.DMA
    return pl.pallas_call(
        functools.partial(kernel, lanes, wides, rate),
        out_shape=jax.ShapeDtypeStruct((rows, width), F32),
        in_specs=[hbm, hbm, hbm, pl.BlockSpec(memory_space=pltpu.SMEM)],
        out_specs=vmem,
        scratch_shapes=[
            pltpu.VMEM((lanes, 8, 128), jnp.int32),
            *[pltpu.VMEM((lanes, rows, block), F32)] * 4,
            pltpu.VMEM((ITERS, lanes, rows, width), F32),
            pltpu.VMEM((ITERS, lanes + 1, rows, width), F32),
            *[pltpu.VMEM((block, width), BF16)] * 4,
            *[pltpu.VMEM((block, block), BF16)] * 2,
            pltpu.VMEM((ITERS, lanes, rows, width), F32),
            pltpu.VMEM((ITERS, steps + 1, rows, width), F32),
            pltpu.VMEM((ITERS, steps, rows, width), F32),
            pltpu.VMEM((ITERS, steps, rows, width), F32),
            pltpu.VMEM((ITERS, lanes, rows, width), F32),
            pltpu.VMEM((ITERS, lanes, rows, width), F32),
            *[pltpu.VMEM((block, block), BF16)] * 2,
            pltpu.VMEM((block, block), F32),
            dma((3,)),
            *[dma((lanes,))] * 6,
            *[dma((ITERS, lanes))] * 2,
            *[dma((ITERS, steps, CHUNKS))] * 4,
            *[dma((ITERS, steps))] * 2,
            *[dma((ITERS, steps, CHUNKS))] * 2,
            *[dma((ITERS, lanes))] * 2,
        ],
        compiler_params=pltpu.CompilerParams(
            collective_id=0, has_side_effects=True, vmem_limit_bytes=54784 * 1024
        ),
        cost_estimate=pl.CostEstimate(
            flops=ITERS * 18 * block * block * width, bytes_accessed=4 * block * block, transcendentals=0
        ),
    )(embeddings, co_engagement, confidence, tile_offset)


def solution(mesh):
    in_specs = (
        P(("wide", "narrow"), None),
        P("wide", "narrow"),
        P("wide", "narrow"),
        P("wide", "narrow"),
    )
    out_specs = P(("wide", "narrow"), None)
    return jax.shard_map(body, mesh=mesh, in_specs=in_specs, out_specs=out_specs, check_vma=False)
```
